32 devices in a mesh: tensor: 2 (over x), dp: 16 (over z, y, core).
Axes of the slice: x: 2, y: 2, z: 4, core: 2. Of those that a mesh axis runs over, the one named last changes fastest.
Arguments:
- inputs: bfloat16 [4096, 8192], P('dp', 'tensor'), may hold values from -6 to 6
- frozen_value_weight: bfloat16 [8192, 1024], P(None, 'tensor'), may hold values from -0.0625 to 0.0625
- adapter_down_matrix: bfloat16 [16, 8192, 16], P('dp', 'tensor'), may hold values from -0.0625 to 0.0625
- adapter_up_matrix: bfloat16 [16, 16, 1024], P('dp', None, 'tensor'), may hold values from -1.5 to 1.5
- value_cotangent: bfloat16 [4096, 1024], P('dp', 'tensor'), may hold values from -6 to 6
- tenant_of_block: int32 [32], P('dp'), may hold values from 0 to 15
- quotas: int32 [16], replicated, may hold values from 128 to 1023
Outputs:
- adapted_values: bfloat16 [4096, 1024], P('dp', 'tensor')
- gradient_inputs: bfloat16 [4096, 8192], P('dp', 'tensor')
- down_grad: float32 [16, 8192, 16], P('dp', 'tensor')
- gradient_up_matrix: float32 [16, 16, 1024], P('dp', None, 'tensor')
The draws below stay inside these ranges and needn't reach their ends.
All inputs are finite; a program needn't handle non-finite values.
Results may differ from the reference program's by a relative error of at most 0.015.
Values may be sent and summed in bfloat16 or wider, within the bound.
No kernel may reach another device: no remote copies, remote signals or barrier semaphores. Data moves between devices by JAX's collectives and lax.ppermute only.
A program may use at most 64 MiB of HBM per device.

```python
import math
import jax
import jax.numpy as jnp
import numpy as np
from jax import lax

MODEL_WIDTH = 8192
VALUE_WIDTH = 1024
ADAPTER_RANK = 16
BLOCK = 128
ADAPTER_TOTAL = 16
TOKEN_TOTAL = 4096
NBLK = 32
N_TENSOR = 2


def place_ends(drawn, key, low, high):
    spot = [jax.random.randint(jax.random.fold_in(key, axis), (), 0, length) for axis, length in enumerate(drawn.shape)]
    longest = drawn.shape.index(max(drawn.shape))
    neighbour = spot[:longest] + [(spot[longest] + 1) % drawn.shape[longest]] + spot[longest + 1:]
    return drawn.at[tuple(spot)].set(low).at[tuple(neighbour)].set(high)


def shard_levels(key, extent, cuts, smallest, top_value):
    loudness, own = 1.0, jax.random.fold_in(key, 6)
    for axis_at, shards_of in cuts:
        heights = jnp.exp(jax.random.uniform(jax.random.fold_in(own, axis_at), (shards_of,), jnp.float32, smallest / len(cuts), top_value / len(cuts)))
        loudness = loudness * jnp.repeat(heights, extent[axis_at] // shards_of).reshape([-1 if axis == axis_at else 1 for axis in range(len(extent))])
    return loudness


def cumulative_ranks(amount, slope):
    weights = [(1 << 20) // math.isqrt(rank ** slope) + 1 for rank in range(1, amount + 1)]
    spread = 1 + sum(weights) // (1 << 30)
    return np.cumsum(np.array([max(1, weight // spread) for weight in weights]))


def ranked_ids(rng, shape, amount, slope):
    table = cumulative_ranks(amount, slope)
    pick = jax.random.randint(jax.random.fold_in(rng, 1), shape, 0, int(table[amount - 1]))
    rank = jnp.searchsorted(jnp.asarray(table, jnp.int32), pick, side="right")
    return jax.random.permutation(jax.random.fold_in(rng, 2), amount)[rank].astype(jnp.int32)


def bell_draw(stream_key, shape, spread, most, cuts=(), held_as=jnp.bfloat16):
    result = jax.random.normal(stream_key, shape, jnp.float32) * spread
    if len(cuts) > 0:
        result = shard_levels(stream_key, shape, cuts, -0.22, 0.18) * result
    return jnp.clip(result, min=-most, max=most).astype(held_as)


def setup_inputs(seed: int = 0) -> dict:
    arg_keys = jax.random.split(jax.random.key(seed), 8)
    return {
        "inputs": bell_draw(arg_keys[0], (TOKEN_TOTAL, MODEL_WIDTH), 1.0, 6.0, ((0, 16), (1, 2))),
        "frozen_value_weight": bell_draw(arg_keys[1], (MODEL_WIDTH, VALUE_WIDTH), MODEL_WIDTH ** -0.5, 0.0625, ((1, 2),)),
        "adapter_down_matrix": bell_draw(arg_keys[2], (ADAPTER_TOTAL, MODEL_WIDTH, ADAPTER_RANK), MODEL_WIDTH ** -0.5, 0.0625, ((0, 16), (1, 2))),
        "adapter_up_matrix": bell_draw(arg_keys[3], (ADAPTER_TOTAL, ADAPTER_RANK, VALUE_WIDTH), ADAPTER_RANK ** -0.5, 1.5, ((0, 16), (2, 2))),
        "value_cotangent": bell_draw(arg_keys[4], (TOKEN_TOTAL, VALUE_WIDTH), 1.0, 6.0, ((0, 16), (1, 2))),
        "tenant_of_block": place_ends(ranked_ids(arg_keys[5], (NBLK,), ADAPTER_TOTAL, 2), jax.random.fold_in(arg_keys[5], 3), 0, ADAPTER_TOTAL - 1).astype(jnp.int32),
        "quotas": place_ends(jax.random.randint(arg_keys[6], (ADAPTER_TOTAL,), BLOCK, 8 * BLOCK), jax.random.fold_in(arg_keys[6], 1), BLOCK, (8 * BLOCK) - 1).astype(jnp.int32),
    }


adapter_scale = 2.0


def reference(inputs, frozen_value_weight, adapter_down_matrix, adapter_up_matrix, value_cotangent, tenant_of_block, quotas):
    nblocks = tenant_of_block.shape[0]
    input_blocks = inputs.reshape(nblocks, BLOCK, MODEL_WIDTH)
    value_grad_blocks = value_cotangent.reshape(nblocks, BLOCK, VALUE_WIDTH)
    frozen_output = jnp.dot(inputs, frozen_value_weight, preferred_element_type=jnp.float32)

    def block_partials(packed):
        x_rows, value_grad_rows, tenant_number = packed
        down_weight = adapter_down_matrix[tenant_number]
        up_weight = adapter_up_matrix[tenant_number]
        reduced_features = jnp.dot(x_rows, down_weight, preferred_element_type=jnp.float32).astype(jnp.bfloat16)
        gradient_lowrank = (adapter_scale * lax.dot_general(value_grad_rows, up_weight, (((1,), (1,)), ((), ())), preferred_element_type=jnp.float32)).astype(jnp.bfloat16)
        raised_output = jnp.dot(reduced_features, up_weight, preferred_element_type=jnp.float32)
        adapter_input = lax.dot_general(gradient_lowrank, down_weight, (((1,), (1,)), ((), ())), preferred_element_type=jnp.float32)
        return reduced_features, gradient_lowrank, raised_output, adapter_input

    reduced_features, gradient_lowrank, raised_output, adapter_input = lax.map(block_partials, (input_blocks, value_grad_blocks, tenant_of_block))
    adapted_values = (frozen_output + adapter_scale * raised_output.reshape(TOKEN_TOTAL, VALUE_WIDTH)).astype(jnp.bfloat16)

    group = VALUE_WIDTH // N_TENSOR

    def add_group(index, running):
        dv_part = lax.dynamic_slice_in_dim(value_cotangent, index * group, group, 1)
        w_part = lax.dynamic_slice_in_dim(frozen_value_weight, index * group, group, 1)
        term = lax.dot_general(dv_part, w_part, (((1,), (1,)), ((), ())), preferred_element_type=jnp.float32)
        return running + term.astype(jnp.bfloat16).astype(jnp.float32)

    summed_gradient = lax.fori_loop(0, N_TENSOR, add_group, jnp.zeros((TOKEN_TOTAL, MODEL_WIDTH), jnp.float32))
    gradient_inputs = (summed_gradient + adapter_input.reshape(TOKEN_TOTAL, MODEL_WIDTH)).astype(jnp.bfloat16)

    onehot = (tenant_of_block[:, None] == jnp.arange(ADAPTER_TOTAL, dtype=jnp.int32)[None, :]).astype(jnp.float32)
    counts = jnp.sum(onehot, axis=0) * BLOCK
    scale = quotas.astype(jnp.float32) / jnp.maximum(counts, 1.0)
    quota_weighted = onehot * scale[None, :]
    grad_a = jnp.einsum('bnd,bnr->bdr', input_blocks.astype(jnp.float32), gradient_lowrank.astype(jnp.float32))
    up_gradient_local = jnp.einsum('bnr,bnk->brk', reduced_features.astype(jnp.float32), value_grad_blocks.astype(jnp.float32))
    down_grad = jnp.einsum('ba,bdr->adr', quota_weighted, grad_a, precision=lax.Precision.HIGHEST)
    gradient_up_matrix = adapter_scale * jnp.einsum('mw,mqf->wqf', quota_weighted, up_gradient_local, precision=lax.Precision.HIGHEST)
    return adapted_values, gradient_inputs, down_grad, gradient_up_matrix
```

```python
import functools

import jax
import jax.numpy as jnp
from jax import lax
from jax.experimental import pallas as pl
from jax.experimental.pallas import tpu as pltpu
from jax.sharding import PartitionSpec as P

ADAPTER_RANK = 16
BLOCK = 128
PIECES = 4
VMEM_LIMIT = 48 * 1024 * 1024

adapter_scale = 2.0

NT = (((1,), (1,)), ((), ()))


def dot(a, b):
    return jnp.dot(a, b, preferred_element_type=jnp.float32)


def dot_nt(a, b):
    return lax.dot_general(a, b, NT, preferred_element_type=jnp.float32)


def own_kernel(t_ref, x_ref, w_ref, cot_ref, v_ref, g_ref, acc):
    step = pl.program_id(0)

    @pl.when(step == 0)
    def _():
        acc[...] = jnp.zeros_like(acc)

    acc[...] += dot(x_ref[...], w_ref[...])
    g_ref[...] = dot_nt(cot_ref[...], w_ref[...]).astype(g_ref.dtype)

    @pl.when(step == pl.num_programs(0) - 1)
    def _():
        v_ref[...] = acc[...]


def own_columns(tensor_index, x, w, cot):
    rows, features = x.shape
    values = w.shape[1]
    chunk = min(1024, features)
    steps = features // chunk
    return pl.pallas_call(
        own_kernel,
        grid_spec=pltpu.PrefetchScalarGridSpec(
            num_scalar_prefetch=1,
            grid=(steps,),
            in_specs=[
                pl.BlockSpec((rows, chunk), lambda j, t: (0, j)),
                pl.BlockSpec((chunk, values), lambda j, t: (t[0] * steps + j, 0)),
                pl.BlockSpec((rows, values), lambda j, t: (0, 0)),
            ],
            out_specs=[
                pl.BlockSpec((rows, values), lambda j, t: (0, 0)),
                pl.BlockSpec((rows, chunk), lambda j, t: (0, j)),
            ],
            scratch_shapes=[pltpu.VMEM((rows, values), jnp.float32)],
        ),
        out_shape=[
            jax.ShapeDtypeStruct((rows, values), jnp.float32),
            jax.ShapeDtypeStruct((rows, features), jnp.bfloat16),
        ],
        compiler_params=pltpu.CompilerParams(vmem_limit_bytes=VMEM_LIMIT),
        cost_estimate=pl.CostEstimate(
            flops=4 * rows * features * values,
            bytes_accessed=2 * features * values + 4 * rows * features,
            transcendentals=0,
        ),
    )(tensor_index, x, w, cot)


def other_values_kernel(parts, chunk, off_ref, x_ref, *refs):
    w_refs, v_ref = refs[:parts], refs[parts]
    total = None
    for k in range(parts):
        at = pl.multiple_of(off_ref[k], chunk)
        term = dot(x_ref[:, pl.ds(at, chunk)], w_refs[k][...])
        total = term if total is None else total + term
    v_ref[...] = total.astype(v_ref.dtype)


def other_values(offsets, x, w_parts):
    rows, features = x.shape
    chunk, values = w_parts[0].shape
    whole = pl.BlockSpec(memory_space=pltpu.VMEM)
    return pl.pallas_call(
        functools.partial(other_values_kernel, len(w_parts), chunk),
        in_specs=[pl.BlockSpec(memory_space=pltpu.SMEM)] + [whole] * (1 + len(w_parts)),
        out_specs=whole,
        out_shape=jax.ShapeDtypeStruct((rows, values), jnp.bfloat16),
        compiler_params=pltpu.CompilerParams(vmem_limit_bytes=VMEM_LIMIT),
        cost_estimate=pl.CostEstimate(
            flops=2 * rows * features * values,
            bytes_accessed=2 * features * (rows + values),
            transcendentals=0,
        ),
    )(offsets, x, *w_parts)


def input_gradient_kernel(groups, parts, chunk, nblocks, off_ref, own_ref, low_ref, down_ref, *refs):
    cot_refs = refs[:groups]
    w_refs = refs[groups : groups + groups * parts]
    out_ref = refs[-1]
    for k in range(parts):
        at = pl.multiple_of(off_ref[k], chunk)
        here = pl.ds(at, chunk)
        total = own_ref[:, here].astype(jnp.float32)
        for group in range(groups):
            term = dot_nt(cot_refs[group][...], w_refs[group * parts + k][...])
            total = total + term.astype(jnp.bfloat16).astype(jnp.float32)
        for b in range(nblocks):
            rows = slice(b * BLOCK, (b + 1) * BLOCK)
            added = total[rows] + dot(low_ref[rows], down_ref[b, :, here])
            out_ref[rows, here] = added.astype(out_ref.dtype)


def input_gradient(offsets, own, grad_low, down_blocks, cots, w_groups):
    rows, features = own.shape
    parts = len(w_groups[0])
    chunk, values = w_groups[0][0].shape
    flat = [w for group in w_groups for w in group]
    whole = pl.BlockSpec(memory_space=pltpu.VMEM)
    return pl.pallas_call(
        functools.partial(
            input_gradient_kernel, len(cots), parts, chunk, down_blocks.shape[0]
        ),
        in_specs=[pl.BlockSpec(memory_space=pltpu.SMEM)] + [whole] * (3 + len(cots) + len(flat)),
        out_specs=whole,
        out_shape=jax.ShapeDtypeStruct((rows, features), jnp.bfloat16),
        compiler_params=pltpu.CompilerParams(vmem_limit_bytes=VMEM_LIMIT),
        cost_estimate=pl.CostEstimate(
            flops=2 * rows * features * values * len(cots),
            bytes_accessed=2 * features * values * len(cots) + 4 * rows * features,
            transcendentals=0,
        ),
    )(offsets, own, grad_low, down_blocks, *cots, *flat)


def on_device(
    inputs,
    frozen_value_weight,
    adapter_down_matrix,
    adapter_up_matrix,
    value_cotangent,
    tenant_of_block,
    quotas,
):
    token_rows, features = inputs.shape
    values = frozen_value_weight.shape[1]
    nblocks = tenant_of_block.shape[0]
    owned = adapter_down_matrix.shape[0]
    n_dp, n_tensor = lax.axis_size("dp"), lax.axis_size("tensor")
    adapter_count = owned * n_dp
    me, t = lax.axis_index("dp"), lax.axis_index("tensor")
    upper = n_dp // 4

    def flip(a, mask):
        return lax.ppermute(a, "dp", [(i, i ^ mask) for i in range(n_dp)])

    def turn(a, shift):
        return lax.ppermute(a, "tensor", [(i, (i + shift) % n_tensor) for i in range(n_tensor)])

    shifts = range(1, n_tensor)

    up_own = adapter_up_matrix.reshape(owned * ADAPTER_RANK, values)
    ids = jnp.zeros((16, values), jnp.bfloat16)
    ids = ids.at[:, :nblocks].set(tenant_of_block.astype(jnp.bfloat16)[None, :])
    message = jnp.concatenate([up_own, ids], axis=0)
    stack = jnp.stack([message] + [flip(message, 4 * m) for m in range(1, upper)])
    stack = jnp.stack([stack, flip(stack, 1)])
    stack = jnp.stack([stack, flip(stack, 2)])
    stack = stack.reshape((n_dp,) + message.shape)

    def place(owner):
        relative = owner ^ me
        return ((relative >> 1) & 1) * (2 * upper) + (relative & 1) * upper + (relative >> 2)

    tenants_rel = stack[:, owned * ADAPTER_RANK, :nblocks].astype(jnp.int32)
    adapter_ids = jnp.arange(adapter_count, dtype=jnp.int32)
    counts = jnp.sum((tenants_rel.reshape(-1)[:, None] == adapter_ids[None, :]).astype(jnp.float32), axis=0)
    scale_all = quotas.astype(jnp.float32) / jnp.maximum(counts * BLOCK, 1.0)
    scale = lax.dynamic_slice_in_dim(scale_all, me * owned, owned)
    partner_tenant = tenants_rel[2 * upper]

    tenant = tenant_of_block
    owner, slot = tenant // owned, tenant % owned
    ups = stack[:, : owned * ADAPTER_RANK].reshape(n_dp * owned, ADAPTER_RANK, values)
    up_blocks = ups[place(owner) * owned + slot]

    cot_blocks = value_cotangent.reshape(nblocks, BLOCK, values)
    grad_part = jnp.einsum("bnk,brk->bnr", cot_blocks, up_blocks, preferred_element_type=jnp.float32)
    grad_sum = grad_part
    for s in shifts:
        grad_sum = grad_sum + turn(grad_part, s)
    grad_low = (adapter_scale * grad_sum).astype(jnp.bfloat16)

    down_own = jnp.swapaxes(adapter_down_matrix, 1, 2)
    down = jnp.stack([down_own] + [flip(down_own, 4 * m) for m in range(1, upper)])
    down = jnp.stack([down, flip(down, 1)])
    down = down.reshape(2 * upper * owned, ADAPTER_RANK, features)

    def near(who):
        o = who // owned
        relative = o ^ me
        return ((relative & 1) * upper + (relative >> 2)) * owned + who % owned

    def on_my_side(who):
        return (((who // owned) ^ me) & 2) == 0

    from_partner = flip(down[near(partner_tenant)], 2)
    down_blocks = jnp.where(on_my_side(tenant)[:, None, None], down[near(tenant)], from_partner)

    input_blocks = inputs.reshape(nblocks, BLOCK, features)
    low_part = jnp.einsum("bnd,brd->bnr", input_blocks, down_blocks, preferred_element_type=jnp.float32)
    low_sum = low_part
    for s in shifts:
        low_sum = low_sum + turn(low_part, s)
    low = low_sum.astype(jnp.bfloat16)

    pieces = PIECES if features % (PIECES * 4 * 128) == 0 else 1
    chunk = features // (pieces * 4)
    offsets, w_groups = [], []
    for s in shifts:
        parts = []
        for p in range(pieces):
            bit = 1 + p % 2
            quarter = ((me >> bit) & 1) * 2 + (me & 1)
            start = ((t + s) % n_tensor) * features + p * 4 * chunk + quarter * chunk
            sent = lax.dynamic_slice_in_dim(frozen_value_weight, start, chunk, 0)
            first = turn(sent, s)
            second = flip(first, 1 << bit)
            both = jnp.stack([first, second])
            crossed = flip(both, 1)
            parts += [first, second, crossed[0], crossed[1]]
            if s == 1:
                offsets += [(p * 4 + (quarter ^ q)) * chunk for q in (0, 2, 1, 3)]
        w_groups.append(parts)
    offsets = jnp.stack(offsets).astype(jnp.int32)
    cots = [turn(value_cotangent, s) for s in shifts]

    value_own, gradient_own = own_columns(t.reshape(1).astype(jnp.int32), inputs, frozen_value_weight, value_cotangent)
    value_sum = value_own
    for s in shifts:
        value_sum = value_sum + turn(other_values(offsets, inputs, w_groups[s - 1]), -s).astype(jnp.float32)
    raised = jnp.einsum("bnr,brk->bnk", low.reshape(nblocks, BLOCK, ADAPTER_RANK), up_blocks, preferred_element_type=jnp.float32)
    adapted_values = (value_sum + adapter_scale * raised.reshape(token_rows, values)).astype(jnp.bfloat16)

    gradient_inputs = input_gradient(
        offsets,
        gradient_own,
        grad_low.reshape(token_rows, ADAPTER_RANK),
        down_blocks,
        cots,
        w_groups,
    )

    down_grad_blocks = jnp.einsum("bnr,bnd->brd", grad_low, input_blocks, preferred_element_type=jnp.float32).astype(jnp.bfloat16)
    partner_blocks = flip(down_grad_blocks, 2)
    four = jnp.concatenate([down_grad_blocks, partner_blocks]).astype(jnp.float32)
    four_tenants = jnp.concatenate([tenant, partner_tenant])
    where = jnp.where(on_my_side(four_tenants), near(four_tenants), -1)
    held = 2 * upper * owned
    weight = (jnp.arange(held, dtype=jnp.int32)[:, None] == where[None, :]).astype(jnp.float32)
    sums = jnp.sum(weight[:, :, None, None] * four[None], axis=1)
    sums = sums.reshape(2, upper, owned, ADAPTER_RANK, features)
    crossed = flip(sums[1].astype(jnp.bfloat16), 1)
    sums = sums[0] + crossed.astype(jnp.float32)
    down_total = sums[0]
    for m in range(1, upper):
        down_total = down_total + flip(sums[m].astype(jnp.bfloat16), 4 * m).astype(jnp.float32)
    down_grad = jnp.swapaxes(down_total * scale[:, None, None], 1, 2)

    up_grad_blocks = adapter_scale * jnp.einsum("bnr,bnk->brk", low, cot_blocks, preferred_element_type=jnp.float32)
    hot = (adapter_ids[:, None] == tenant[None, :]).astype(jnp.float32)
    dense = jnp.sum(hot[:, :, None, None] * up_grad_blocks[None], axis=1).astype(jnp.bfloat16)
    received = lax.all_to_all(dense, "dp", split_axis=0, concat_axis=0, tiled=True)
    received = received.reshape(n_dp, owned, ADAPTER_RANK, values).astype(jnp.float32)
    gradient_up_matrix = jnp.sum(received, axis=0) * scale[:, None, None]
    return (adapted_values, gradient_inputs, down_grad, gradient_up_matrix)


def solution(mesh):
    placed = (
        P("dp", "tensor"),
        P(None, "tensor"),
        P("dp", "tensor", None),
        P("dp", None, "tensor"),
        P("dp", "tensor"),
        P("dp"),
        P(),
    )
    return jax.shard_map(
        on_device,
        mesh=mesh,
        in_specs=placed,
        out_specs=(
            P("dp", "tensor"),
            P("dp", "tensor"),
            P("dp", "tensor", None),
            P("dp", None, "tensor"),
        ),
        check_vma=False,
    )
```

```python
import functools

import jax
import jax.numpy as jnp
from jax import lax
from jax.experimental import pallas as pl
from jax.experimental.pallas import tpu as pltpu
from jax.sharding import PartitionSpec as P

RANK = 16
BLOCK = 128
PIECES = 2
HOPPING = 2
HALVES = 2
COUNT = 128
VMEM_LIMIT = 20 * 1024 * 1024

adapter_scale = 2.0

NT = (((1,), (1,)), ((), ()))
TN = (((0,), (0,)), ((), ()))

f32, bf16 = jnp.float32, jnp.bfloat16


def dot(a, b):
    return jnp.dot(a, b, preferred_element_type=f32)


def dot_nt(a, b):
    return lax.dot_general(a, b, NT, preferred_element_type=f32)


def dot_tn(a, b):
    return lax.dot_general(a, b, TN, preferred_element_type=f32)


SMEM = pl.BlockSpec(memory_space=pltpu.SMEM)
VMEM = pl.BlockSpec(memory_space=pltpu.VMEM)
HBM = pl.BlockSpec(memory_space=pltpu.HBM)


def call(kernel, in_specs, out_shape, out_specs, args, scratch=(), flops=0, moved=1 << 20, limit=VMEM_LIMIT, **settings):
    return pl.pallas_call(
        functools.partial(kernel, **settings),
        in_specs=in_specs,
        out_specs=out_specs,
        out_shape=out_shape,
        scratch_shapes=list(scratch),
        compiler_params=pltpu.CompilerParams(vmem_limit_bytes=limit),
        cost_estimate=pl.CostEstimate(flops=0, bytes_accessed=0, transcendentals=0),
    )(*args)


def like(shape, dtype):
    return jax.ShapeDtypeStruct(shape, dtype)


def message_kernel(down, up, message, sem):
    features = down.shape[2]
    copies = [
        pltpu.make_async_copy(down, message.at[:, :, pl.ds(0, features)], sem.at[0]),
        pltpu.make_async_copy(up, message.at[:, :, pl.ds(features, up.shape[2])], sem.at[1]),
    ]
    for copy in copies:
        copy.start()
    for copy in copies:
        copy.wait()


def weights_kernel(w, *refs, features, chunk, pieces, n_tensor):
    sent, sem = refs[:-1], refs[-1]
    t, me = lax.axis_index("tensor"), lax.axis_index("dp")
    copies = []
    for k, out in enumerate(sent):
        s, p = k // pieces + 1, k % pieces
        start = lax.rem(t + s, n_tensor) * features + first_row(me, p, 0, chunk)
        copies.append(pltpu.make_async_copy(w.at[pl.ds(pl.multiple_of(start, chunk), out.shape[0])], out, sem.at[k]))
    for copy in copies:
        copy.start()
    for copy in copies:
        copy.wait()


def first_row(me, p, q, chunk):
    if p < HOPPING:
        part = (((me >> 2) & 1) * 2 + (me & 1)) ^ q
    else:
        part = ((me & 1) ^ q) * 2
    return (p * 4 + part) * chunk


def part_offset(me, k, chunk):
    p, q = (k // 4, (0, 2, 1, 3)[k % 4]) if k < 4 * HOPPING else (HOPPING + (k - 4 * HOPPING) // 2, k % 2)
    return pl.multiple_of(first_row(me, p, q, chunk), chunk)


def near(who, me, upper, owned):
    relative = (who // owned) ^ me
    return ((relative & 1) * upper + (relative >> 2)) * owned + lax.rem(who, owned)


def on_my_side(who, me, owned):
    return (((who // owned) ^ me) & 2) == 0


def select_kernel(here, tenant, partner, *refs, upper, owned):
    held, (mine, partners) = refs[:-2], refs[-2:]
    me = here[1]
    for b in range(tenant.shape[0]):
        for who, out in ((partner[b], partners), (tenant[b], mine)):
            at = near(who, me, upper, owned)
            for k, group in enumerate(held):
                for o in range(owned):

                    @pl.when(at == k * owned + o)
                    def _(group=group, o=o, out=out, b=b):
                        out[b] = group[o]


def low_kernel(here, tenant, x, cot, mine, theirs, blocks, part, *, owned):
    me, features = here[1], x.shape[1]
    nblocks = tenant.shape[0]
    for b in range(nblocks):
        mine_here = on_my_side(tenant[b], me, owned)

        @pl.when(mine_here)
        def _(b=b):
            blocks[b] = mine[b]

        @pl.when(jnp.logical_not(mine_here))
        def _(b=b):
            blocks[b] = theirs[b]

        rows = slice(b * BLOCK, (b + 1) * BLOCK)
        part[b] = dot_nt(blocks[b, :, :features], x[rows, :])
        part[nblocks + b] = dot_nt(blocks[b, :, features:], cot[rows, :])


def gradient_kernel(x, cot, *refs):
    parts, (low, grad_low, out) = refs[:-3], refs[-3:]
    nblocks, features, values = low.shape[0], x.shape[1], cot.shape[1]
    for b in range(nblocks):
        low_sum, grad_sum = parts[0][b], parts[0][nblocks + b]
        for part in parts[1:]:
            low_sum, grad_sum = low_sum + part[b], grad_sum + part[nblocks + b]
        rows = slice(b * BLOCK, (b + 1) * BLOCK)
        low[b] = low_sum.astype(bf16)
        grad_low[b] = (adapter_scale * grad_sum).astype(bf16)
        out[b, :, :features] = dot(grad_low[b], x[rows, :]).astype(bf16)
        out[b, :, features : features + values] = (adapter_scale * dot(low[b], cot[rows, :])).astype(bf16)
        out[b, :, features + values :] = jnp.ones((RANK, COUNT), bf16)


def spread_kernel(here, tenant, partner, mine, theirs, keep, send, acc, *, upper, owned):
    me = here[1]
    acc[...] = jnp.zeros_like(acc)
    for b in range(tenant.shape[0]):
        for who, source in ((tenant[b], mine), (partner[b], theirs)):

            @pl.when(on_my_side(who, me, owned))
            def _(who=who, source=source, b=b):
                at = near(who, me, upper, owned)
                acc[at] = acc[at] + source[b].astype(f32)

    half = upper * owned
    keep[...] = acc[:half]
    send[...] = acc[half:].astype(bf16)


def cross_kernel(keep, received, first, *rest, owned):
    for o in range(owned):
        first[o] = keep[o] + received[o].astype(f32)
    for m, out in enumerate(rest, 1):
        for o in range(owned):
            out[o] = (keep[m * owned + o] + received[m * owned + o].astype(f32)).astype(bf16)


def final_kernel(here, quotas, first, *refs, owned):
    others, (down_grad, up_grad) = refs[:-2], refs[-2:]
    features, values = down_grad.shape[2], up_grad.shape[2]
    for o in range(owned):
        total = first[o]
        for other in others:
            total = total + other[o].astype(f32)
        rows = jnp.maximum(total[:, features + values : features + values + 1] * BLOCK, 1.0)
        scale = jnp.full(rows.shape, quotas[here[1] * owned + o]).astype(f32) / rows
        down_grad[o] = total[:, :features] * scale
        up_grad[o] = total[:, features : features + values] * scale


def own_values_kernel(here, x_ref, w_ref, out_ref):
    @pl.when(pl.program_id(0) == 0)
    def _():
        out_ref[...] = jnp.zeros_like(out_ref)

    out_ref[...] += dot(x_ref[...], w_ref[...])


def own_gradient_kernel(here, cot_ref, w_ref, out_ref):
    out_ref[...] = dot_nt(cot_ref[...], w_ref[...]).astype(out_ref.dtype)


def own_columns(kernel, here, a, a_spec, w, out_shape, out_spec, features, chunk):
    steps = features // chunk
    return pl.pallas_call(
        kernel,
        grid_spec=pltpu.PrefetchScalarGridSpec(
            num_scalar_prefetch=1,
            grid=(steps,),
            in_specs=[a_spec, pl.BlockSpec((chunk, w.shape[1]), lambda j, here: (here[0] * steps + j, 0))],
            out_specs=out_spec,
        ),
        out_shape=out_shape,
        compiler_params=pltpu.CompilerParams(vmem_limit_bytes=57 * 1024 * 1024),
        cost_estimate=pl.CostEstimate(flops=0, bytes_accessed=0, transcendentals=0),
    )(here, a, w)


def other_values_kernel(here, x, *refs, chunk):
    w_refs, outs = refs[:-HALVES], refs[-HALVES:]
    total = None
    for k, w in enumerate(w_refs):
        term = dot(x[:, pl.ds(part_offset(here[1], k, chunk), w.shape[0])], w[...])
        total = term if total is None else total + term
    width = outs[0].shape[1]
    for i, out in enumerate(outs):
        out[...] = total[:, i * width : (i + 1) * width].astype(out.dtype)


def input_gradient_kernel(here, own, grad_low, blocks, *refs, groups, parts, chunk):
    cots, ws, out = refs[:groups], refs[groups:-1], refs[-1]
    for k in range(parts):
        span = pl.ds(part_offset(here[1], k, chunk), ws[k].shape[0])
        total = own[:, span].astype(f32)
        for group in range(groups):
            term = dot_nt(cots[group][...], ws[group * parts + k][...])
            total = total + term.astype(bf16).astype(f32)
        for b in range(grad_low.shape[0]):
            rows = slice(b * BLOCK, (b + 1) * BLOCK)
            out[rows, span] = (total[rows] + dot_tn(grad_low[b], blocks[b, :, span])).astype(out.dtype)


def values_kernel(own, low, blocks, *refs):
    received, out = refs[:-1], refs[-1]
    features = blocks.shape[2] - own.shape[1]
    for b in range(low.shape[0]):
        rows = slice(b * BLOCK, (b + 1) * BLOCK)
        total = own[rows] + adapter_scale * dot_tn(low[b], blocks[b, :, features:])
        for i in range(HALVES):
            width = received[i].shape[1]
            span = slice(i * width, (i + 1) * width)
            part = total[:, span]
            for other in received[i::HALVES]:
                part = part + other[rows].astype(f32)
            out[rows, span] = part.astype(out.dtype)


def after(a, *first):
    return lax.optimization_barrier((a, *first))[0]


def on_device(
    inputs,
    frozen_value_weight,
    adapter_down_matrix,
    adapter_up_matrix,
    value_cotangent,
    tenant_of_block,
    quotas,
):
    token_rows, features = inputs.shape
    values = frozen_value_weight.shape[1]
    nblocks = tenant_of_block.shape[0]
    owned = adapter_down_matrix.shape[0]
    n_dp, n_tensor = lax.axis_size("dp"), lax.axis_size("tensor")
    upper = n_dp // 4
    shifts = range(1, n_tensor)
    here = jnp.stack([lax.axis_index("tensor"), lax.axis_index("dp")]).astype(jnp.int32)
    tenant = tenant_of_block

    def flip(a, mask):
        return lax.ppermute(a, "dp", [(i, i ^ mask) for i in range(n_dp)])

    def turn(a, shift):
        return lax.ppermute(a, "tensor", [(i, (i + shift) % n_tensor) for i in range(n_tensor)])

    def turns(a):
        return [turn(a, s) for s in shifts]

    pieces = PIECES if features % (PIECES * 4 * 128) == 0 else 1
    chunk = features // (pieces * 4)
    n_sent = len(shifts) * pieces
    width = features + values
    message = call(
        message_kernel,
        [HBM, HBM],
        like((owned, RANK, width), bf16),
        VMEM,
        (jnp.swapaxes(adapter_down_matrix, 1, 2), adapter_up_matrix),
        scratch=[pltpu.SemaphoreType.DMA((2,))],
        limit=52 * 1024 * 1024,
    )
    sent = call(
        weights_kernel,
        [HBM],
        [like((chunk * (1 if k % pieces < HOPPING else 2), values), bf16) for k in range(n_sent)],
        [VMEM] * n_sent,
        (frozen_value_weight,),
        scratch=[pltpu.SemaphoreType.DMA((n_sent,))],
        limit=52 * 1024 * 1024,
        features=features,
        chunk=chunk,
        pieces=pieces,
        n_tensor=n_tensor,
    )
    adapters = [message] + [flip(message, 4 * m) for m in range(1, upper)]
    first_w = [turn(sent[k], k // pieces + 1) for k in range(n_sent)]
    partner = flip(after(tenant, message), 2)

    def hopping(arrays):
        return [a for k, a in enumerate(arrays) if k % pieces < HOPPING]

    def of_piece(p):
        return [k for k in range(n_sent) if k % pieces == p]

    own_chunk = min(1024, features)
    rows_by_chunk = pl.BlockSpec((token_rows, own_chunk), lambda j, here: (0, j))
    rows_by_values = pl.BlockSpec((token_rows, values), lambda j, here: (0, 0))

    def own(kernel, at, a, a_spec, out_shape, out_spec):
        return own_columns(kernel, at, a, a_spec, frozen_value_weight, out_shape, out_spec, features, own_chunk)

    value_own = own(
        own_values_kernel,
        after(here, partner),
        inputs,
        rows_by_chunk,
        like((token_rows, values), f32),
        rows_by_values,
    )

    held = adapters + [flip(after(a, value_own), 1) for a in adapters]
    mine, partners = call(
        select_kernel,
        [SMEM, SMEM, SMEM] + [VMEM] * len(held),
        [like((nblocks, RANK, width), bf16)] * 2,
        [VMEM, VMEM],
        (here, tenant, after(partner, *[first_w[k] for k in of_piece(0)]), *held),
        upper=upper,
        owned=owned,
    )
    def hop(p, *first):
        return {k: flip(after(first_w[k], *first), 4) for k in of_piece(p) if p < HOPPING}

    hops = hop(0, partners)
    blocks, part = call(
        low_kernel,
        [SMEM, SMEM, VMEM, VMEM, VMEM, VMEM],
        [like((nblocks, RANK, width), bf16), like((2 * nblocks, RANK, BLOCK), f32)],
        [VMEM, VMEM],
        (here, tenant, inputs, value_cotangent, mine, flip(partners, 2)),
        owned=owned,
    )
    parts = [part] + turns(part)
    for p in range(1, pieces):
        hops.update(hop(p, part))
    low, grad_low, gradients = call(
        gradient_kernel,
        [VMEM] * (2 + len(parts)),
        [like((nblocks, RANK, BLOCK), bf16)] * 2 + [like((nblocks, RANK, width + COUNT), bf16)],
        [VMEM] * 3,
        (inputs, after(value_cotangent, *[hops[k] for k in of_piece(0)]), *parts),
    )

    cots = turns(after(value_cotangent, gradients))

    gradient_own = own(
        own_gradient_kernel,
        after(here, gradients),
        value_cotangent,
        rows_by_values,
        like((token_rows, features), bf16),
        rows_by_chunk,
    )

    keep, crossing = call(
        spread_kernel,
        [SMEM, SMEM, SMEM, VMEM, VMEM],
        [like((upper * owned, RANK, width + COUNT), f32), like((upper * owned, RANK, width + COUNT), bf16)],
        [VMEM, VMEM],
        (here, tenant, after(partner, gradient_own, *cots), gradients, flip(gradients, 2)),
        scratch=[pltpu.VMEM((2 * upper * owned, RANK, width + COUNT), f32)],
        upper=upper,
        owned=owned,
    )

    summed, *to_owners = call(
        cross_kernel,
        [VMEM, VMEM],
        [like((owned, RANK, width + COUNT), f32)] + [like((owned, RANK, width + COUNT), bf16)] * (upper - 1),
        [VMEM] * upper,
        (keep, after(flip(crossing, 1), *[hops[k] for k in of_piece(1) if k in hops])),
        owned=owned,
    )
    owners = [flip(a, 4 * m) for m, a in enumerate(to_owners, 1)]

    w_groups = []
    for s in shifts:
        group = []
        for k in range((s - 1) * pieces, s * pieces):
            held_here = [first_w[k], hops[k]] if k in hops else [first_w[k]]
            group += held_here + [flip(after(a, gradients), 1) for a in held_here]
        w_groups.append(group)
    value_parts = []
    for s in shifts:
        value_part = call(
            other_values_kernel,
            [SMEM, VMEM] + [VMEM] * len(w_groups[s - 1]),
            [like((token_rows, values // HALVES), bf16)] * HALVES,
            [VMEM] * HALVES,
            (after(here, summed), inputs, *w_groups[s - 1]),
            flops=2 * token_rows * features * values,
            moved=2 * features * (token_rows + values),
            chunk=chunk,
        )
        value_parts += value_part

    flat = [w for group in w_groups for w in group]
    gradient_inputs = call(
        input_gradient_kernel,
        [SMEM] + [VMEM] * (3 + len(cots) + len(flat)),
        like((token_rows, features), bf16),
        VMEM,
        (after(here, *value_parts), gradient_own, grad_low, blocks, *cots, *flat),
        flops=2 * token_rows * features * values * len(cots),
        moved=2 * features * values * len(cots) + 4 * token_rows * features,
        groups=len(cots),
        parts=len(w_groups[0]),
        chunk=chunk,
    )
    returned = [turn(a, -(i // HALVES + 1)) for i, a in enumerate(value_parts)]
    adapted_values = call(
        values_kernel,
        [VMEM] * (3 + len(returned)),
        like((token_rows, values), bf16),
        VMEM,
        (value_own, low, blocks, *returned),
    )
    down_grad, gradient_up_matrix = call(
        final_kernel,
        [SMEM, SMEM] + [VMEM] * upper,
        [like((owned, RANK, features), f32), like((owned, RANK, values), f32)],
        [VMEM, VMEM],
        (here, after(quotas, adapted_values), summed, *owners),
        moved=1 << 26,
        owned=owned,
    )
    return (adapted_values, gradient_inputs, jnp.swapaxes(down_grad, 1, 2), gradient_up_matrix)


def solution(mesh):
    placed = (
        P("dp", "tensor"),
        P(None, "tensor"),
        P("dp", "tensor", None),
        P("dp", None, "tensor"),
        P("dp", "tensor"),
        P("dp"),
        P(),
    )
    return jax.shard_map(
        on_device,
        mesh=mesh,
        in_specs=placed,
        out_specs=(
            P("dp", "tensor"),
            P("dp", "tensor"),
            P("dp", "tensor", None),
            P("dp", None, "tensor"),
        ),
        check_vma=False,
    )
```

```python
import functools

import jax
import jax.numpy as jnp
from jax import lax
from jax.experimental import pallas as pl
from jax.experimental.pallas import tpu as pltpu
from jax.sharding import PartitionSpec as P

RANK = 16
BLOCK = 128
PIECES = 2
HOPPING = 2
HALVES = 2
OWN_STEPS = 4
COUNT = 128
VMEM_LIMIT = 20 * 1024 * 1024

adapter_scale = 2.0

NT = (((1,), (1,)), ((), ()))
TN = (((0,), (0,)), ((), ()))

f32, bf16 = jnp.float32, jnp.bfloat16


def dot(a, b):
    return jnp.dot(a, b, preferred_element_type=f32)


def dot_nt(a, b):
    return lax.dot_general(a, b, NT, preferred_element_type=f32)


def dot_tn(a, b):
    return lax.dot_general(a, b, TN, preferred_element_type=f32)


SMEM = pl.BlockSpec(memory_space=pltpu.SMEM)
VMEM = pl.BlockSpec(memory_space=pltpu.VMEM)
HBM = pl.BlockSpec(memory_space=pltpu.HBM)


def call(kernel, in_specs, out_shape, out_specs, args, scratch=(), flops=0, moved=1 << 20, limit=VMEM_LIMIT, **settings):
    return pl.pallas_call(
        functools.partial(kernel, **settings),
        in_specs=in_specs,
        out_specs=out_specs,
        out_shape=out_shape,
        scratch_shapes=list(scratch),
        compiler_params=pltpu.CompilerParams(vmem_limit_bytes=limit),
        cost_estimate=pl.CostEstimate(flops=0, bytes_accessed=0, transcendentals=0),
    )(*args)


def like(shape, dtype):
    return jax.ShapeDtypeStruct(shape, dtype)


def message_kernel(down, up, message, sem):
    features = down.shape[2]
    copies = [
        pltpu.make_async_copy(down, message.at[:, :, pl.ds(0, features)], sem.at[0]),
        pltpu.make_async_copy(up, message.at[:, :, pl.ds(features, up.shape[2])], sem.at[1]),
    ]
    for copy in copies:
        copy.start()
    for copy in copies:
        copy.wait()


def weights_kernel(w, *refs, features, chunk, pieces, n_tensor):
    sent, sem = refs[:-1], refs[-1]
    t, me = lax.axis_index("tensor"), lax.axis_index("dp")
    copies = []
    for k, out in enumerate(sent):
        s, p = k // pieces + 1, k % pieces
        start = lax.rem(t + s, n_tensor) * features + first_row(me, p, 0, chunk)
        copies.append(pltpu.make_async_copy(w.at[pl.ds(pl.multiple_of(start, chunk), out.shape[0])], out, sem.at[k]))
    for copy in copies:
        copy.start()
    for copy in copies:
        copy.wait()


def first_row(me, p, q, chunk):
    if p < HOPPING:
        part = (((me >> 2) & 1) * 2 + (me & 1)) ^ q
    else:
        part = ((me & 1) ^ q) * 2
    return (p * 4 + part) * chunk


def part_offset(me, k, chunk):
    p, q = (k // 4, (0, 2, 1, 3)[k % 4]) if k < 4 * HOPPING else (HOPPING + (k - 4 * HOPPING) // 2, k % 2)
    return pl.multiple_of(first_row(me, p, q, chunk), chunk)


def near(who, me, upper, owned):
    relative = (who // owned) ^ me
    return ((relative & 1) * upper + (relative >> 2)) * owned + lax.rem(who, owned)


def on_my_side(who, me, owned):
    return (((who // owned) ^ me) & 2) == 0


def select_kernel(here, tenant, partner, *refs, upper, owned):
    held, (mine, partners) = refs[:-2], refs[-2:]
    me = here[1]
    for b in range(tenant.shape[0]):
        for who, out in ((partner[b], partners), (tenant[b], mine)):
            at = near(who, me, upper, owned)
            for k, group in enumerate(held):
                for o in range(owned):

                    @pl.when(at == k * owned + o)
                    def _(group=group, o=o, out=out, b=b):
                        out[b] = group[o]


def low_kernel(here, tenant, x, cot, mine, theirs, blocks, part, *, owned):
    me, features = here[1], x.shape[1]
    nblocks = tenant.shape[0]
    for b in range(nblocks):
        mine_here = on_my_side(tenant[b], me, owned)

        @pl.when(mine_here)
        def _(b=b):
            blocks[b] = mine[b]

        @pl.when(jnp.logical_not(mine_here))
        def _(b=b):
            blocks[b] = theirs[b]

    both = blocks[...].reshape(nblocks * RANK, blocks.shape[2])
    lows = dot_nt(x[...], both[:, :features])
    grads = dot_nt(cot[...], both[:, features:])
    for b in range(nblocks):
        rows, ranks = slice(b * BLOCK, (b + 1) * BLOCK), slice(b * RANK, (b + 1) * RANK)
        part[b] = lows[rows, ranks].T
        part[nblocks + b] = grads[rows, ranks].T


def gradient_kernel(x, cot, *refs):
    parts, (low, grad_low, out) = refs[:-3], refs[-3:]
    nblocks, features, values = low.shape[0], x.shape[1], cot.shape[1]
    for b in range(nblocks):
        low_sum, grad_sum = parts[0][b], parts[0][nblocks + b]
        for part in parts[1:]:
            low_sum, grad_sum = low_sum + part[b], grad_sum + part[nblocks + b]
        rows = slice(b * BLOCK, (b + 1) * BLOCK)
        low[b] = low_sum.astype(bf16)
        grad_low[b] = (adapter_scale * grad_sum).astype(bf16)
        out[b, :, :features] = dot(grad_low[b], x[rows, :]).astype(bf16)
        out[b, :, features : features + values] = (adapter_scale * dot(low[b], cot[rows, :])).astype(bf16)
        out[b, :, features + values :] = jnp.ones((RANK, COUNT), bf16)


def spread_kernel(here, tenant, partner, mine, theirs, keep, send, acc, *, upper, owned):
    me = here[1]
    acc[...] = jnp.zeros_like(acc)
    for b in range(tenant.shape[0]):
        for who, source in ((tenant[b], mine), (partner[b], theirs)):

            @pl.when(on_my_side(who, me, owned))
            def _(who=who, source=source, b=b):
                at = near(who, me, upper, owned)
                acc[at] = acc[at] + source[b].astype(f32)

    half = upper * owned
    keep[...] = acc[:half]
    send[...] = acc[half:].astype(bf16)


def cross_kernel(keep, received, first, *rest, owned):
    for o in range(owned):
        first[o] = keep[o] + received[o].astype(f32)
    for m, out in enumerate(rest, 1):
        for o in range(owned):
            out[o] = (keep[m * owned + o] + received[m * owned + o].astype(f32)).astype(bf16)


def final_kernel(here, quotas, first, *refs, owned):
    others, (down_grad, up_grad) = refs[:-2], refs[-2:]
    features, values = down_grad.shape[2], up_grad.shape[2]
    for o in range(owned):
        total = first[o]
        for other in others:
            total = total + other[o].astype(f32)
        rows = jnp.maximum(total[:, features + values : features + values + 1] * BLOCK, 1.0)
        scale = jnp.full(rows.shape, quotas[here[1] * owned + o]).astype(f32) / rows
        down_grad[o] = total[:, :features] * scale
        up_grad[o] = total[:, features : features + values] * scale


def own_weights(here, w, held, sem):
    steps, chunk, _ = held.shape
    copies = []
    for j in range(steps):
        start = pl.multiple_of(here[0] * (steps * chunk) + j * chunk, chunk)
        copies.append(pltpu.make_async_copy(w.at[pl.ds(start, chunk)], held.at[j], sem.at[j]))
        copies[-1].start()
    for j in range(steps):
        copies[j].wait()
        yield slice(j * chunk, (j + 1) * chunk), held[j]


def own_values_kernel(here, x, w, out, held, sem):
    total = None
    for span, part in own_weights(here, w, held, sem):
        term = dot(x[:, span], part)
        total = term if total is None else total + term
    out[...] = total


def own_gradient_kernel(here, cot, w, out, held, sem):
    for span, part in own_weights(here, w, held, sem):
        out[:, span] = dot_nt(cot[...], part).astype(out.dtype)


def other_values_kernel(here, x, *refs, chunk):
    w_refs, outs = refs[:-HALVES], refs[-HALVES:]
    total = None
    for k, w in enumerate(w_refs):
        term = dot(x[:, pl.ds(part_offset(here[1], k, chunk), w.shape[0])], w[...])
        total = term if total is None else total + term
    width = outs[0].shape[1]
    for i, out in enumerate(outs):
        out[...] = total[:, i * width : (i + 1) * width].astype(out.dtype)


def input_gradient_kernel(here, own, grad_low, blocks, *refs, groups, parts, chunk):
    cots, ws, out = refs[:groups], refs[groups:-1], refs[-1]
    for k in range(parts):
        span = pl.ds(part_offset(here[1], k, chunk), ws[k].shape[0])
        total = own[:, span].astype(f32)
        for group in range(groups):
            term = dot_nt(cots[group][...], ws[group * parts + k][...])
            total = total + term.astype(bf16).astype(f32)
        for b in range(grad_low.shape[0]):
            rows = slice(b * BLOCK, (b + 1) * BLOCK)
            out[rows, span] = (total[rows] + dot_tn(grad_low[b], blocks[b, :, span])).astype(out.dtype)


def values_kernel(own, low, blocks, *refs):
    received, out = refs[:-1], refs[-1]
    features = blocks.shape[2] - own.shape[1]
    for b in range(low.shape[0]):
        rows = slice(b * BLOCK, (b + 1) * BLOCK)
        total = own[rows] + adapter_scale * dot_tn(low[b], blocks[b, :, features:])
        for i in range(HALVES):
            width = received[i].shape[1]
            span = slice(i * width, (i + 1) * width)
            part = total[:, span]
            for other in received[i::HALVES]:
                part = part + other[rows].astype(f32)
            out[rows, span] = part.astype(out.dtype)


def after(a, *first):
    return lax.optimization_barrier((a, *first))[0]


def on_device(
    inputs,
    frozen_value_weight,
    adapter_down_matrix,
    adapter_up_matrix,
    value_cotangent,
    tenant_of_block,
    quotas,
):
    token_rows, features = inputs.shape
    values = frozen_value_weight.shape[1]
    nblocks = tenant_of_block.shape[0]
    owned = adapter_down_matrix.shape[0]
    n_dp, n_tensor = lax.axis_size("dp"), lax.axis_size("tensor")
    upper = n_dp // 4
    shifts = range(1, n_tensor)
    here = jnp.stack([lax.axis_index("tensor"), lax.axis_index("dp")]).astype(jnp.int32)
    tenant = tenant_of_block

    def flip(a, mask):
        return lax.ppermute(a, "dp", [(i, i ^ mask) for i in range(n_dp)])

    def turn(a, shift):
        return lax.ppermute(a, "tensor", [(i, (i + shift) % n_tensor) for i in range(n_tensor)])

    def turns(a):
        return [turn(a, s) for s in shifts]

    pieces = PIECES if features % (PIECES * 4 * 128) == 0 else 1
    chunk = features // (pieces * 4)
    n_sent = len(shifts) * pieces
    width = features + values
    message = call(
        message_kernel,
        [HBM, HBM],
        like((owned, RANK, width), bf16),
        VMEM,
        (jnp.swapaxes(adapter_down_matrix, 1, 2), adapter_up_matrix),
        scratch=[pltpu.SemaphoreType.DMA((2,))],
        limit=52 * 1024 * 1024,
    )
    sent = call(
        weights_kernel,
        [HBM],
        [like((chunk * (1 if k % pieces < HOPPING else 2), values), bf16) for k in range(n_sent)],
        [VMEM] * n_sent,
        (frozen_value_weight,),
        scratch=[pltpu.SemaphoreType.DMA((n_sent,))],
        limit=52 * 1024 * 1024,
        features=features,
        chunk=chunk,
        pieces=pieces,
        n_tensor=n_tensor,
    )
    adapters = [message] + [flip(message, 4 * m) for m in range(1, upper)]
    first_w = [turn(sent[k], k // pieces + 1) for k in range(n_sent)]
    partner = flip(after(tenant, message), 2)

    def hopping(arrays):
        return [a for k, a in enumerate(arrays) if k % pieces < HOPPING]

    def of_piece(p):
        return [k for k in range(n_sent) if k % pieces == p]

    own_steps = OWN_STEPS if features % (OWN_STEPS * 128) == 0 else 1

    def own(kernel, at, a, out_shape):
        return call(
            kernel,
            [SMEM, VMEM, HBM],
            out_shape,
            VMEM,
            (at, a, frozen_value_weight),
            scratch=[
                pltpu.VMEM((own_steps, features // own_steps, values), bf16),
                pltpu.SemaphoreType.DMA((own_steps,)),
            ],
            limit=52 * 1024 * 1024,
        )


    held = adapters + [flip(a, 1) for a in adapters]
    mine, partners = call(
        select_kernel,
        [SMEM, SMEM, SMEM] + [VMEM] * len(held),
        [like((nblocks, RANK, width), bf16)] * 2,
        [VMEM, VMEM],
        (here, tenant, partner, *held),
        upper=upper,
        owned=owned,
    )
    def hop(p, *first):
        return {k: flip(after(first_w[k], *first), 4) for k in of_piece(p) if p < HOPPING}

    hops = hop(0, *adapters)
    value_own = own(own_values_kernel, after(here, partners), inputs, like((token_rows, values), f32))
    blocks, part = call(
        low_kernel,
        [SMEM, SMEM, VMEM, VMEM, VMEM, VMEM],
        [like((nblocks, RANK, width), bf16), like((2 * nblocks, RANK, BLOCK), f32)],
        [VMEM, VMEM],
        (here, after(tenant, value_own), inputs, value_cotangent, mine, flip(partners, 2)),
        owned=owned,
    )
    parts = [part] + turns(part)
    for p in range(1, pieces):
        hops.update(hop(p, part))
    low, grad_low, gradients = call(
        gradient_kernel,
        [VMEM] * (2 + len(parts)),
        [like((nblocks, RANK, BLOCK), bf16)] * 2 + [like((nblocks, RANK, width + COUNT), bf16)],
        [VMEM] * 3,
        (inputs, after(value_cotangent, *[hops[k] for k in of_piece(0)]), *parts),
    )

    cots = turns(after(value_cotangent, gradients))

    gradient_own = own(
        own_gradient_kernel, after(here, gradients), value_cotangent, like((token_rows, features), bf16)
    )

    keep, crossing = call(
        spread_kernel,
        [SMEM, SMEM, SMEM, VMEM, VMEM],
        [like((upper * owned, RANK, width + COUNT), f32), like((upper * owned, RANK, width + COUNT), bf16)],
        [VMEM, VMEM],
        (here, tenant, after(partner, gradient_own, *cots), gradients, flip(gradients, 2)),
        scratch=[pltpu.VMEM((2 * upper * owned, RANK, width + COUNT), f32)],
        upper=upper,
        owned=owned,
    )

    summed, *to_owners = call(
        cross_kernel,
        [VMEM, VMEM],
        [like((owned, RANK, width + COUNT), f32)] + [like((owned, RANK, width + COUNT), bf16)] * (upper - 1),
        [VMEM] * upper,
        (keep, after(flip(crossing, 1), *[hops[k] for k in of_piece(1) if k in hops])),
        owned=owned,
    )
    owners = [flip(a, 4 * m) for m, a in enumerate(to_owners, 1)]

    w_groups = []
    for s in shifts:
        group = []
        for k in range((s - 1) * pieces, s * pieces):
            held_here = [first_w[k], hops[k]] if k in hops else [first_w[k]]
            group += held_here + [flip(after(a, gradients), 1) for a in held_here]
        w_groups.append(group)
    value_parts = []
    for s in shifts:
        value_part = call(
            other_values_kernel,
            [SMEM, VMEM] + [VMEM] * len(w_groups[s - 1]),
            [like((token_rows, values // HALVES), bf16)] * HALVES,
            [VMEM] * HALVES,
            (after(here, summed), inputs, *w_groups[s - 1]),
            flops=2 * token_rows * features * values,
            moved=2 * features * (token_rows + values),
            chunk=chunk,
        )
        value_parts += value_part

    flat = [w for group in w_groups for w in group]
    gradient_inputs = call(
        input_gradient_kernel,
        [SMEM] + [VMEM] * (3 + len(cots) + len(flat)),
        like((token_rows, features), bf16),
        VMEM,
        (after(here, *value_parts), gradient_own, grad_low, blocks, *cots, *flat),
        flops=2 * token_rows * features * values * len(cots),
        moved=2 * features * values * len(cots) + 4 * token_rows * features,
        groups=len(cots),
        parts=len(w_groups[0]),
        chunk=chunk,
    )
    returned = [turn(a, -(i // HALVES + 1)) for i, a in enumerate(value_parts)]
    adapted_values = call(
        values_kernel,
        [VMEM] * (3 + len(returned)),
        like((token_rows, values), bf16),
        VMEM,
        (value_own, low, blocks, *returned),
    )
    down_grad, gradient_up_matrix = call(
        final_kernel,
        [SMEM, SMEM] + [VMEM] * upper,
        [like((owned, RANK, features), f32), like((owned, RANK, values), f32)],
        [VMEM, VMEM],
        (here, after(quotas, adapted_values), summed, *owners),
        moved=1 << 26,
        owned=owned,
    )
    return (adapted_values, gradient_inputs, jnp.swapaxes(down_grad, 1, 2), gradient_up_matrix)


def solution(mesh):
    placed = (
        P("dp", "tensor"),
        P(None, "tensor"),
        P("dp", "tensor", None),
        P("dp", None, "tensor"),
        P("dp", "tensor"),
        P("dp"),
        P(),
    )
    return jax.shard_map(
        on_device,
        mesh=mesh,
        in_specs=placed,
        out_specs=(
            P("dp", "tensor"),
            P("dp", "tensor"),
            P("dp", "tensor", None),
            P("dp", None, "tensor"),
        ),
        check_vma=False,
    )
```

```python
import functools

import jax
import jax.numpy as jnp
from jax import lax
from jax.experimental import pallas as pl
from jax.experimental.pallas import tpu as pltpu
from jax.sharding import PartitionSpec as P

RANK = 16
BLOCK = 128
PIECES = 2
HOPPING = 2
HALVES = 2
OWN_STEPS = 8
COUNT = 128
VMEM_LIMIT = 20 * 1024 * 1024

adapter_scale = 2.0

NT = (((1,), (1,)), ((), ()))
TN = (((0,), (0,)), ((), ()))

f32, bf16 = jnp.float32, jnp.bfloat16


def dot(a, b):
    return jnp.dot(a, b, preferred_element_type=f32)


def dot_nt(a, b):
    return lax.dot_general(a, b, NT, preferred_element_type=f32)


def dot_tn(a, b):
    return lax.dot_general(a, b, TN, preferred_element_type=f32)


SMEM = pl.BlockSpec(memory_space=pltpu.SMEM)
VMEM = pl.BlockSpec(memory_space=pltpu.VMEM)
HBM = pl.BlockSpec(memory_space=pltpu.HBM)


def call(kernel, in_specs, out_shape, out_specs, args, scratch=(), flops=0, moved=1 << 20, limit=VMEM_LIMIT, **settings):
    return pl.pallas_call(
        functools.partial(kernel, **settings),
        in_specs=in_specs,
        out_specs=out_specs,
        out_shape=out_shape,
        scratch_shapes=list(scratch),
        compiler_params=pltpu.CompilerParams(vmem_limit_bytes=limit),
        cost_estimate=pl.CostEstimate(flops=0, bytes_accessed=0, transcendentals=0),
    )(*args)


def like(shape, dtype):
    return jax.ShapeDtypeStruct(shape, dtype)


def message_kernel(down, up, message, sem):
    features = down.shape[2]
    copies = [
        pltpu.make_async_copy(down, message.at[:, :, pl.ds(0, features)], sem.at[0]),
        pltpu.make_async_copy(up, message.at[:, :, pl.ds(features, up.shape[2])], sem.at[1]),
    ]
    for copy in copies:
        copy.start()
    for copy in copies:
        copy.wait()


def weights_kernel(w, *refs, features, chunk, pieces, n_tensor):
    sent, sem = refs[:-1], refs[-1]
    t, me = lax.axis_index("tensor"), lax.axis_index("dp")
    copies = []
    for k, out in enumerate(sent):
        s, p = k // pieces + 1, k % pieces
        start = lax.rem(t + s, n_tensor) * features + first_row(me, p, 0, chunk)
        copies.append(pltpu.make_async_copy(w.at[pl.ds(pl.multiple_of(start, chunk), out.shape[0])], out, sem.at[k]))
    for copy in copies:
        copy.start()
    for copy in copies:
        copy.wait()


def first_row(me, p, q, chunk):
    if p < HOPPING:
        part = (((me >> 2) & 1) * 2 + (me & 1)) ^ q
    else:
        part = ((me & 1) ^ q) * 2
    return (p * 4 + part) * chunk


def part_offset(me, k, chunk):
    p, q = (k // 4, (0, 2, 1, 3)[k % 4]) if k < 4 * HOPPING else (HOPPING + (k - 4 * HOPPING) // 2, k % 2)
    return pl.multiple_of(first_row(me, p, q, chunk), chunk)


def near(who, me, upper, owned):
    relative = (who // owned) ^ me
    return ((relative & 1) * upper + (relative >> 2)) * owned + lax.rem(who, owned)


def on_my_side(who, me, owned):
    return (((who // owned) ^ me) & 2) == 0


def select_kernel(here, tenant, partner, *refs, upper, owned):
    held, (mine, partners) = refs[:-2], refs[-2:]
    me = here[1]
    for b in range(tenant.shape[0]):
        for who, out in ((partner[b], partners), (tenant[b], mine)):
            at = near(who, me, upper, owned)
            for k, group in enumerate(held):
                for o in range(owned):

                    @pl.when(at == k * owned + o)
                    def _(group=group, o=o, out=out, b=b):
                        out[b] = group[o]


def low_kernel(here, tenant, x, cot, mine, theirs, blocks, part, *, owned):
    me, features = here[1], x.shape[1]
    nblocks = tenant.shape[0]
    for b in range(nblocks):
        mine_here = on_my_side(tenant[b], me, owned)

        @pl.when(mine_here)
        def _(b=b):
            blocks[b] = mine[b]

        @pl.when(jnp.logical_not(mine_here))
        def _(b=b):
            blocks[b] = theirs[b]

    both = blocks[...].reshape(nblocks * RANK, blocks.shape[2])
    lows = dot_nt(x[...], both[:, :features])
    grads = dot_nt(cot[...], both[:, features:])
    for b in range(nblocks):
        rows, ranks = slice(b * BLOCK, (b + 1) * BLOCK), slice(b * RANK, (b + 1) * RANK)
        part[b] = lows[rows, ranks].T
        part[nblocks + b] = grads[rows, ranks].T


def gradient_kernel(x, cot, *refs):
    parts, (low, grad_low, out) = refs[:-3], refs[-3:]
    nblocks, features, values = low.shape[0], x.shape[1], cot.shape[1]
    for b in range(nblocks):
        low_sum, grad_sum = parts[0][b], parts[0][nblocks + b]
        for part in parts[1:]:
            low_sum, grad_sum = low_sum + part[b], grad_sum + part[nblocks + b]
        rows = slice(b * BLOCK, (b + 1) * BLOCK)
        low[b] = low_sum.astype(bf16)
        grad_low[b] = (adapter_scale * grad_sum).astype(bf16)
        out[b, :, :features] = dot(grad_low[b], x[rows, :]).astype(bf16)
        out[b, :, features : features + values] = (adapter_scale * dot(low[b], cot[rows, :])).astype(bf16)
        out[b, :, features + values :] = jnp.ones((RANK, COUNT), bf16)


def spread_kernel(here, tenant, partner, mine, theirs, keep, send, acc, *, upper, owned):
    me = here[1]
    acc[...] = jnp.zeros_like(acc)
    for b in range(tenant.shape[0]):
        for who, source in ((tenant[b], mine), (partner[b], theirs)):

            @pl.when(on_my_side(who, me, owned))
            def _(who=who, source=source, b=b):
                at = near(who, me, upper, owned)
                acc[at] = acc[at] + source[b].astype(f32)

    half = upper * owned
    keep[...] = acc[:half]
    send[...] = acc[half:].astype(bf16)


def cross_kernel(keep, received, first, *rest, owned):
    for o in range(owned):
        first[o] = keep[o] + received[o].astype(f32)
    for m, out in enumerate(rest, 1):
        for o in range(owned):
            out[o] = (keep[m * owned + o] + received[m * owned + o].astype(f32)).astype(bf16)


def final_kernel(here, quotas, first, *refs, owned):
    others, (down_grad, up_grad) = refs[:-2], refs[-2:]
    features, values = down_grad.shape[2], up_grad.shape[2]
    for o in range(owned):
        total = first[o]
        for other in others:
            total = total + other[o].astype(f32)
        rows = jnp.maximum(total[:, features + values : features + values + 1] * BLOCK, 1.0)
        scale = jnp.full(rows.shape, quotas[here[1] * owned + o]).astype(f32) / rows
        down_grad[o] = total[:, :features] * scale
        up_grad[o] = total[:, features : features + values] * scale


def own_weights(here, w, held, sem):
    steps, chunk, _ = held.shape
    copies = []
    for j in range(steps):
        start = pl.multiple_of(here[0] * (steps * chunk) + j * chunk, chunk)
        copies.append(pltpu.make_async_copy(w.at[pl.ds(start, chunk)], held.at[j], sem.at[j]))
        copies[-1].start()
    for j in range(steps):
        copies[j].wait()
        yield slice(j * chunk, (j + 1) * chunk), held[j]


def own_values_kernel(here, x, w, out, held, sem):
    total = None
    for span, part in own_weights(here, w, held, sem):
        term = dot(x[:, span], part)
        total = term if total is None else total + term
    out[...] = total


def own_gradient_kernel(here, cot, w, out, held, sem):
    for span, part in own_weights(here, w, held, sem):
        out[:, span] = dot_nt(cot[...], part).astype(out.dtype)


def other_values_kernel(here, x, *refs, chunk):
    w_refs, outs = refs[:-HALVES], refs[-HALVES:]
    total = None
    for k, w in enumerate(w_refs):
        term = dot(x[:, pl.ds(part_offset(here[1], k, chunk), w.shape[0])], w[...])
        total = term if total is None else total + term
    width = outs[0].shape[1]
    for i, out in enumerate(outs):
        out[...] = total[:, i * width : (i + 1) * width].astype(out.dtype)


def input_gradient_kernel(here, own, grad_low, blocks, *refs, groups, parts, chunk):
    cots, ws, out = refs[:groups], refs[groups:-1], refs[-1]
    for k in range(parts):
        span = pl.ds(part_offset(here[1], k, chunk), ws[k].shape[0])
        total = own[:, span].astype(f32)
        for group in range(groups):
            term = dot_nt(cots[group][...], ws[group * parts + k][...])
            total = total + term.astype(bf16).astype(f32)
        for b in range(grad_low.shape[0]):
            rows = slice(b * BLOCK, (b + 1) * BLOCK)
            out[rows, span] = (total[rows] + dot_tn(grad_low[b], blocks[b, :, span])).astype(out.dtype)


def values_kernel(own, low, blocks, *refs):
    received, out = refs[:-1], refs[-1]
    features = blocks.shape[2] - own.shape[1]
    for b in range(low.shape[0]):
        rows = slice(b * BLOCK, (b + 1) * BLOCK)
        total = own[rows] + adapter_scale * dot_tn(low[b], blocks[b, :, features:])
        for i in range(HALVES):
            width = received[i].shape[1]
            span = slice(i * width, (i + 1) * width)
            part = total[:, span]
            for other in received[i::HALVES]:
                part = part + other[rows].astype(f32)
            out[rows, span] = part.astype(out.dtype)


def after(a, *first):
    return lax.optimization_barrier((a, *first))[0]


def on_device(
    inputs,
    frozen_value_weight,
    adapter_down_matrix,
    adapter_up_matrix,
    value_cotangent,
    tenant_of_block,
    quotas,
):
    token_rows, features = inputs.shape
    values = frozen_value_weight.shape[1]
    nblocks = tenant_of_block.shape[0]
    owned = adapter_down_matrix.shape[0]
    n_dp, n_tensor = lax.axis_size("dp"), lax.axis_size("tensor")
    upper = n_dp // 4
    shifts = range(1, n_tensor)
    here = jnp.stack([lax.axis_index("tensor"), lax.axis_index("dp")]).astype(jnp.int32)
    tenant = tenant_of_block

    def flip(a, mask):
        return lax.ppermute(a, "dp", [(i, i ^ mask) for i in range(n_dp)])

    def turn(a, shift):
        return lax.ppermute(a, "tensor", [(i, (i + shift) % n_tensor) for i in range(n_tensor)])

    def turns(a):
        return [turn(a, s) for s in shifts]

    pieces = PIECES if features % (PIECES * 4 * 128) == 0 else 1
    chunk = features // (pieces * 4)
    n_sent = len(shifts) * pieces
    width = features + values
    message = call(
        message_kernel,
        [HBM, HBM],
        like((owned, RANK, width), bf16),
        VMEM,
        (jnp.swapaxes(adapter_down_matrix, 1, 2), adapter_up_matrix),
        scratch=[pltpu.SemaphoreType.DMA((2,))],
        limit=52 * 1024 * 1024,
    )
    sent = call(
        weights_kernel,
        [HBM],
        [like((chunk * (1 if k % pieces < HOPPING else 2), values), bf16) for k in range(n_sent)],
        [VMEM] * n_sent,
        (frozen_value_weight,),
        scratch=[pltpu.SemaphoreType.DMA((n_sent,))],
        limit=52 * 1024 * 1024,
        features=features,
        chunk=chunk,
        pieces=pieces,
        n_tensor=n_tensor,
    )
    adapters = {0: message}
    for bit in reversed(range(upper.bit_length() - 1)):
        adapters.update({m | 1 << bit: flip(a, 4 << bit) for m, a in adapters.items()})
    adapters = [adapters[m] for m in range(upper)]
    first_w = [turn(sent[k], k // pieces + 1) for k in range(n_sent)]
    partner = flip(after(tenant, message), 2)

    def hopping(arrays):
        return [a for k, a in enumerate(arrays) if k % pieces < HOPPING]

    def of_piece(p):
        return [k for k in range(n_sent) if k % pieces == p]

    own_steps = OWN_STEPS if features % (OWN_STEPS * 128) == 0 else 1

    def own(kernel, at, a, out_shape):
        return call(
            kernel,
            [SMEM, VMEM, HBM],
            out_shape,
            VMEM,
            (at, a, frozen_value_weight),
            scratch=[
                pltpu.VMEM((own_steps, features // own_steps, values), bf16),
                pltpu.SemaphoreType.DMA((own_steps,)),
            ],
            limit=52 * 1024 * 1024,
        )


    held = adapters + [flip(after(a, partner), 1) for a in adapters]
    mine, partners = call(
        select_kernel,
        [SMEM, SMEM, SMEM] + [VMEM] * len(held),
        [like((nblocks, RANK, width), bf16)] * 2,
        [VMEM, VMEM],
        (here, tenant, partner, *held),
        upper=upper,
        owned=owned,
    )
    def hop(p, *first):
        return {k: flip(after(first_w[k], *first), 4) for k in of_piece(p) if p < HOPPING}

    hops = hop(0, adapters[1], partner)
    value_own = own(own_values_kernel, after(here, partners), inputs, like((token_rows, values), f32))
    for p in range(1, pieces):
        hops.update(hop(p, value_own))
    blocks, part = call(
        low_kernel,
        [SMEM, SMEM, VMEM, VMEM, VMEM, VMEM],
        [like((nblocks, RANK, width), bf16), like((2 * nblocks, RANK, BLOCK), f32)],
        [VMEM, VMEM],
        (here, after(tenant, value_own), inputs, value_cotangent, mine, flip(partners, 2)),
        owned=owned,
    )
    parts = [part] + turns(part)
    low, grad_low, gradients = call(
        gradient_kernel,
        [VMEM] * (2 + len(parts)),
        [like((nblocks, RANK, BLOCK), bf16)] * 2 + [like((nblocks, RANK, width + COUNT), bf16)],
        [VMEM] * 3,
        (inputs, after(value_cotangent, *[hops[k] for k in of_piece(0)]), *parts),
    )

    cots = turns(after(value_cotangent, gradients))

    gradient_own = own(
        own_gradient_kernel, after(here, gradients), value_cotangent, like((token_rows, features), bf16)
    )

    keep, crossing = call(
        spread_kernel,
        [SMEM, SMEM, SMEM, VMEM, VMEM],
        [like((upper * owned, RANK, width + COUNT), f32), like((upper * owned, RANK, width + COUNT), bf16)],
        [VMEM, VMEM],
        (here, tenant, after(partner, gradient_own, *cots), gradients, flip(gradients, 2)),
        scratch=[pltpu.VMEM((2 * upper * owned, RANK, width + COUNT), f32)],
        upper=upper,
        owned=owned,
    )

    summed, *to_owners = call(
        cross_kernel,
        [VMEM, VMEM],
        [like((owned, RANK, width + COUNT), f32)] + [like((owned, RANK, width + COUNT), bf16)] * (upper - 1),
        [VMEM] * upper,
        (keep, after(flip(crossing, 1), *[hops[k] for k in of_piece(1) if k in hops])),
        owned=owned,
    )
    owners = [flip(a, 4 * m) for m, a in enumerate(to_owners, 1)]

    w_groups = []
    for s in shifts:
        group = []
        for k in range((s - 1) * pieces, s * pieces):
            held_here = [first_w[k], hops[k]] if k in hops else [first_w[k]]
            group += held_here + [flip(after(a, gradients), 1) for a in held_here]
        w_groups.append(group)
    value_parts = []
    for s in shifts:
        value_part = call(
            other_values_kernel,
            [SMEM, VMEM] + [VMEM] * len(w_groups[s - 1]),
            [like((token_rows, values // HALVES), bf16)] * HALVES,
            [VMEM] * HALVES,
            (after(here, summed), inputs, *w_groups[s - 1]),
            flops=2 * token_rows * features * values,
            moved=2 * features * (token_rows + values),
            chunk=chunk,
        )
        value_parts += value_part

    flat = [w for group in w_groups for w in group]
    gradient_inputs = call(
        input_gradient_kernel,
        [SMEM] + [VMEM] * (3 + len(cots) + len(flat)),
        like((token_rows, features), bf16),
        VMEM,
        (after(here, *value_parts), gradient_own, grad_low, blocks, *cots, *flat),
        flops=2 * token_rows * features * values * len(cots),
        moved=2 * features * values * len(cots) + 4 * token_rows * features,
        groups=len(cots),
        parts=len(w_groups[0]),
        chunk=chunk,
    )
    returned = [turn(a, -(i // HALVES + 1)) for i, a in enumerate(value_parts)]
    adapted_values = call(
        values_kernel,
        [VMEM] * (3 + len(returned)),
        like((token_rows, values), bf16),
        VMEM,
        (value_own, low, blocks, *returned),
    )
    down_grad, gradient_up_matrix = call(
        final_kernel,
        [SMEM, SMEM] + [VMEM] * upper,
        [like((owned, RANK, features), f32), like((owned, RANK, values), f32)],
        [VMEM, VMEM],
        (here, after(quotas, adapted_values), summed, *owners),
        moved=1 << 26,
        owned=owned,
    )
    return (adapted_values, gradient_inputs, jnp.swapaxes(down_grad, 1, 2), gradient_up_matrix)


def solution(mesh):
    placed = (
        P("dp", "tensor"),
        P(None, "tensor"),
        P("dp", "tensor", None),
        P("dp", None, "tensor"),
        P("dp", "tensor"),
        P("dp"),
        P(),
    )
    return jax.shard_map(
        on_device,
        mesh=mesh,
        in_specs=placed,
        out_specs=(
            P("dp", "tensor"),
            P("dp", "tensor"),
            P("dp", "tensor", None),
            P("dp", None, "tensor"),
        ),
        check_vma=False,
    )
```

```python
import functools

import jax
import jax.numpy as jnp
from jax import lax
from jax.experimental import pallas as pl
from jax.experimental.pallas import tpu as pltpu
from jax.sharding import PartitionSpec as P

RANK = 16
BLOCK = 128
PIECES = 2
HOPPING = 2
HALVES = 2
OWN_STEPS = 8
COUNT = 128
VMEM_LIMIT = 20 * 1024 * 1024

adapter_scale = 2.0

NT = (((1,), (1,)), ((), ()))
TN = (((0,), (0,)), ((), ()))

f32, bf16 = jnp.float32, jnp.bfloat16


def dot(a, b):
    return jnp.dot(a, b, preferred_element_type=f32)


def dot_nt(a, b):
    return lax.dot_general(a, b, NT, preferred_element_type=f32)


def dot_tn(a, b):
    return lax.dot_general(a, b, TN, preferred_element_type=f32)


SMEM = pl.BlockSpec(memory_space=pltpu.SMEM)
VMEM = pl.BlockSpec(memory_space=pltpu.VMEM)
HBM = pl.BlockSpec(memory_space=pltpu.HBM)


def call(kernel, in_specs, out_shape, out_specs, args, scratch=(), flops=0, moved=1 << 20, limit=VMEM_LIMIT, **settings):
    return pl.pallas_call(
        functools.partial(kernel, **settings),
        in_specs=in_specs,
        out_specs=out_specs,
        out_shape=out_shape,
        scratch_shapes=list(scratch),
        compiler_params=pltpu.CompilerParams(vmem_limit_bytes=limit),
        cost_estimate=pl.CostEstimate(flops=0, bytes_accessed=0, transcendentals=0),
    )(*args)


def like(shape, dtype):
    return jax.ShapeDtypeStruct(shape, dtype)


def message_kernel(down, up, message, sem):
    features = down.shape[2]
    copies = [
        pltpu.make_async_copy(down, message.at[:, :, pl.ds(0, features)], sem.at[0]),
        pltpu.make_async_copy(up, message.at[:, :, pl.ds(features, up.shape[2])], sem.at[1]),
    ]
    for copy in copies:
        copy.start()
    for copy in copies:
        copy.wait()


def weights_kernel(w, *refs, features, chunk, pieces, n_tensor):
    sent, sem = refs[:-1], refs[-1]
    t, me = lax.axis_index("tensor"), lax.axis_index("dp")
    copies = []
    for k, out in enumerate(sent):
        s, p = k // pieces + 1, k % pieces
        start = lax.rem(t + s, n_tensor) * features + first_row(me, p, 0, chunk)
        copies.append(pltpu.make_async_copy(w.at[pl.ds(pl.multiple_of(start, chunk), out.shape[0])], out, sem.at[k]))
    for copy in copies:
        copy.start()
    for copy in copies:
        copy.wait()


def first_row(me, p, q, chunk):
    if p < HOPPING:
        part = (((me >> 2) & 1) * 2 + (me & 1)) ^ q
    else:
        part = ((me & 1) ^ q) * 2
    return (p * 4 + part) * chunk


def part_offset(me, k, chunk):
    p, q = (k // 4, (0, 2, 1, 3)[k % 4]) if k < 4 * HOPPING else (HOPPING + (k - 4 * HOPPING) // 2, k % 2)
    return pl.multiple_of(first_row(me, p, q, chunk), chunk)


def near(who, me, upper, owned):
    relative = (who // owned) ^ me
    return ((relative & 1) * upper + (relative >> 2)) * owned + lax.rem(who, owned)


def on_my_side(who, me, owned):
    return (((who // owned) ^ me) & 2) == 0


def select_kernel(here, tenant, partner, *refs, upper, owned):
    held, (mine, partners) = refs[:-2], refs[-2:]
    me = here[1]
    for b in range(tenant.shape[0]):
        for who, out in ((partner[b], partners), (tenant[b], mine)):
            at = near(who, me, upper, owned)
            for k, group in enumerate(held):
                for o in range(owned):

                    @pl.when(at == k * owned + o)
                    def _(group=group, o=o, out=out, b=b):
                        out[b] = group[o]


def low_kernel(here, tenant, x, cot, mine, theirs, blocks, part, *, owned):
    me, features = here[1], x.shape[1]
    nblocks = tenant.shape[0]
    for b in range(nblocks):
        mine_here = on_my_side(tenant[b], me, owned)

        @pl.when(mine_here)
        def _(b=b):
            blocks[b] = mine[b]

        @pl.when(jnp.logical_not(mine_here))
        def _(b=b):
            blocks[b] = theirs[b]

    both = blocks[...].reshape(nblocks * RANK, blocks.shape[2])
    lows = dot_nt(x[...], both[:, :features])
    grads = dot_nt(cot[...], both[:, features:])
    for b in range(nblocks):
        rows, ranks = slice(b * BLOCK, (b + 1) * BLOCK), slice(b * RANK, (b + 1) * RANK)
        part[b] = lows[rows, ranks].T
        part[nblocks + b] = grads[rows, ranks].T


def gradient_kernel(x, cot, *refs):
    parts, (low, grad_low, out) = refs[:-3], refs[-3:]
    nblocks, features, values = low.shape[0], x.shape[1], cot.shape[1]
    for b in range(nblocks):
        low_sum, grad_sum = parts[0][b], parts[0][nblocks + b]
        for part in parts[1:]:
            low_sum, grad_sum = low_sum + part[b], grad_sum + part[nblocks + b]
        rows = slice(b * BLOCK, (b + 1) * BLOCK)
        low[b] = low_sum.astype(bf16)
        grad_low[b] = (adapter_scale * grad_sum).astype(bf16)
        out[b, :, :features] = dot(grad_low[b], x[rows, :]).astype(bf16)
        out[b, :, features : features + values] = (adapter_scale * dot(low[b], cot[rows, :])).astype(bf16)
        out[b, :, features + values :] = jnp.ones((RANK, COUNT), bf16)


def spread_kernel(here, tenant, partner, mine, theirs, keep, send, acc, *, upper, owned):
    me = here[1]
    acc[...] = jnp.zeros_like(acc)
    for b in range(tenant.shape[0]):
        for who, source in ((tenant[b], mine), (partner[b], theirs)):

            @pl.when(on_my_side(who, me, owned))
            def _(who=who, source=source, b=b):
                at = near(who, me, upper, owned)
                acc[at] = acc[at] + source[b].astype(f32)

    half = upper * owned
    keep[...] = acc[:half]
    send[...] = acc[half:].astype(bf16)


def cross_kernel(keep, received, first, *rest, owned):
    for o in range(owned):
        first[o] = keep[o] + received[o].astype(f32)
    for m, out in enumerate(rest, 1):
        for o in range(owned):
            out[o] = (keep[m * owned + o] + received[m * owned + o].astype(f32)).astype(bf16)


def final_kernel(here, quotas, first, *refs, owned):
    others, (down_grad, up_grad) = refs[:-2], refs[-2:]
    features, values = down_grad.shape[2], up_grad.shape[2]
    for o in range(owned):
        total = first[o]
        for other in others:
            total = total + other[o].astype(f32)
        rows = jnp.maximum(total[:, features + values : features + values + 1] * BLOCK, 1.0)
        scale = jnp.full(rows.shape, quotas[here[1] * owned + o]).astype(f32) / rows
        down_grad[o] = total[:, :features] * scale
        up_grad[o] = total[:, features : features + values] * scale


def own_weights(here, w, held, sem):
    steps, chunk, _ = held.shape
    copies = []
    for j in range(steps):
        start = pl.multiple_of(here[0] * (steps * chunk) + j * chunk, chunk)
        copies.append(pltpu.make_async_copy(w.at[pl.ds(start, chunk)], held.at[j], sem.at[j]))
        copies[-1].start()
    for j in range(steps):
        copies[j].wait()
        yield slice(j * chunk, (j + 1) * chunk), held[j]


def own_values_kernel(here, x, w, out, held, sem):
    total = None
    for span, part in own_weights(here, w, held, sem):
        term = dot(x[:, span], part)
        total = term if total is None else total + term
    out[...] = total


def own_gradient_kernel(here, cot, w, out, held, sem):
    for span, part in own_weights(here, w, held, sem):
        out[:, span] = dot_nt(cot[...], part).astype(out.dtype)


def other_values_kernel(here, x, *refs, chunk):
    w_refs, outs = refs[:-HALVES], refs[-HALVES:]
    total = None
    for k, w in enumerate(w_refs):
        term = dot(x[:, pl.ds(part_offset(here[1], k, chunk), w.shape[0])], w[...])
        total = term if total is None else total + term
    width = outs[0].shape[1]
    for i, out in enumerate(outs):
        out[...] = total[:, i * width : (i + 1) * width].astype(out.dtype)


def input_gradient_kernel(here, own, grad_low, blocks, *refs, groups, parts, chunk):
    cots, ws, out = refs[:groups], refs[groups:-1], refs[-1]
    for k in range(parts):
        span = pl.ds(part_offset(here[1], k, chunk), ws[k].shape[0])
        total = own[:, span].astype(f32)
        for group in range(groups):
            term = dot_nt(cots[group][...], ws[group * parts + k][...])
            total = total + term.astype(bf16).astype(f32)
        for b in range(grad_low.shape[0]):
            rows = slice(b * BLOCK, (b + 1) * BLOCK)
            out[rows, span] = (total[rows] + dot_tn(grad_low[b], blocks[b, :, span])).astype(out.dtype)


def values_kernel(own, low, blocks, *refs):
    received, out = refs[:-1], refs[-1]
    features = blocks.shape[2] - own.shape[1]
    for b in range(low.shape[0]):
        rows = slice(b * BLOCK, (b + 1) * BLOCK)
        total = own[rows] + adapter_scale * dot_tn(low[b], blocks[b, :, features:])
        for i in range(HALVES):
            width = received[i].shape[1]
            span = slice(i * width, (i + 1) * width)
            part = total[:, span]
            for other in received[i::HALVES]:
                part = part + other[rows].astype(f32)
            out[rows, span] = part.astype(out.dtype)


def last_kernel(own, low, blocks, *refs, owned, n_returned):
    returned, (here, quotas, *sums) = refs[:n_returned], refs[n_returned:-3]
    out, down_grad, up_grad = refs[-3:]
    values_kernel(own, low, blocks, *returned, out)
    final_kernel(here, quotas, *sums, down_grad, up_grad, owned=owned)


def after(a, *first):
    return lax.optimization_barrier((a, *first))[0]


def on_device(
    inputs,
    frozen_value_weight,
    adapter_down_matrix,
    adapter_up_matrix,
    value_cotangent,
    tenant_of_block,
    quotas,
):
    token_rows, features = inputs.shape
    values = frozen_value_weight.shape[1]
    nblocks = tenant_of_block.shape[0]
    owned = adapter_down_matrix.shape[0]
    n_dp, n_tensor = lax.axis_size("dp"), lax.axis_size("tensor")
    upper = n_dp // 4
    shifts = range(1, n_tensor)
    here = jnp.stack([lax.axis_index("tensor"), lax.axis_index("dp")]).astype(jnp.int32)
    tenant = tenant_of_block

    def flip(a, mask):
        return lax.ppermute(a, "dp", [(i, i ^ mask) for i in range(n_dp)])

    def turn(a, shift):
        return lax.ppermute(a, "tensor", [(i, (i + shift) % n_tensor) for i in range(n_tensor)])

    def turns(a):
        return [turn(a, s) for s in shifts]

    pieces = PIECES if features % (PIECES * 4 * 128) == 0 else 1
    chunk = features // (pieces * 4)
    n_sent = len(shifts) * pieces
    width = features + values
    message = call(
        message_kernel,
        [HBM, HBM],
        like((owned, RANK, width), bf16),
        VMEM,
        (jnp.swapaxes(adapter_down_matrix, 1, 2), adapter_up_matrix),
        scratch=[pltpu.SemaphoreType.DMA((2,))],
        limit=52 * 1024 * 1024,
    )
    sent = call(
        weights_kernel,
        [HBM],
        [like((chunk * (1 if k % pieces < HOPPING else 2), values), bf16) for k in range(n_sent)],
        [VMEM] * n_sent,
        (frozen_value_weight,),
        scratch=[pltpu.SemaphoreType.DMA((n_sent,))],
        limit=52 * 1024 * 1024,
        features=features,
        chunk=chunk,
        pieces=pieces,
        n_tensor=n_tensor,
    )
    adapters = {0: message}
    for bit in reversed(range(upper.bit_length() - 1)):
        adapters.update({m | 1 << bit: flip(a, 4 << bit) for m, a in adapters.items()})
    adapters = [adapters[m] for m in range(upper)]
    first_w = [turn(sent[k], k // pieces + 1) for k in range(n_sent)]
    partner = flip(after(tenant, message), 2)

    def hopping(arrays):
        return [a for k, a in enumerate(arrays) if k % pieces < HOPPING]

    def of_piece(p):
        return [k for k in range(n_sent) if k % pieces == p]

    own_steps = OWN_STEPS if features % (OWN_STEPS * 128) == 0 else 1

    def own(kernel, at, a, out_shape):
        return call(
            kernel,
            [SMEM, VMEM, HBM],
            out_shape,
            VMEM,
            (at, a, frozen_value_weight),
            scratch=[
                pltpu.VMEM((own_steps, features // own_steps, values), bf16),
                pltpu.SemaphoreType.DMA((own_steps,)),
            ],
            limit=52 * 1024 * 1024,
        )


    held = adapters + [flip(after(a, partner), 1) for a in adapters]
    mine, partners = call(
        select_kernel,
        [SMEM, SMEM, SMEM] + [VMEM] * len(held),
        [like((nblocks, RANK, width), bf16)] * 2,
        [VMEM, VMEM],
        (here, tenant, partner, *held),
        upper=upper,
        owned=owned,
    )
    def hop(p, *first):
        return {k: flip(after(first_w[k], *first), 4) for k in of_piece(p) if p < HOPPING}

    hops = hop(0, adapters[1], partner)
    value_own = own(own_values_kernel, after(here, partners), inputs, like((token_rows, values), f32))
    for p in range(1, pieces):
        hops.update(hop(p, value_own))
    blocks, part = call(
        low_kernel,
        [SMEM, SMEM, VMEM, VMEM, VMEM, VMEM],
        [like((nblocks, RANK, width), bf16), like((2 * nblocks, RANK, BLOCK), f32)],
        [VMEM, VMEM],
        (here, after(tenant, value_own), inputs, value_cotangent, mine, flip(partners, 2)),
        owned=owned,
    )
    parts = [part] + turns(part)
    low, grad_low, gradients = call(
        gradient_kernel,
        [VMEM] * (2 + len(parts)),
        [like((nblocks, RANK, BLOCK), bf16)] * 2 + [like((nblocks, RANK, width + COUNT), bf16)],
        [VMEM] * 3,
        (inputs, after(value_cotangent, *[hops[k] for k in of_piece(0)]), *parts),
    )

    cots = turns(after(value_cotangent, gradients))

    gradient_own = own(
        own_gradient_kernel, after(here, gradients), value_cotangent, like((token_rows, features), bf16)
    )

    keep, crossing = call(
        spread_kernel,
        [SMEM, SMEM, SMEM, VMEM, VMEM],
        [like((upper * owned, RANK, width + COUNT), f32), like((upper * owned, RANK, width + COUNT), bf16)],
        [VMEM, VMEM],
        (here, tenant, after(partner, gradient_own, *cots), gradients, flip(gradients, 2)),
        scratch=[pltpu.VMEM((2 * upper * owned, RANK, width + COUNT), f32)],
        upper=upper,
        owned=owned,
    )

    summed, *to_owners = call(
        cross_kernel,
        [VMEM, VMEM],
        [like((owned, RANK, width + COUNT), f32)] + [like((owned, RANK, width + COUNT), bf16)] * (upper - 1),
        [VMEM] * upper,
        (keep, after(flip(crossing, 1), *[hops[k] for k in of_piece(1) if k in hops])),
        owned=owned,
    )
    owners = [flip(a, 4 * m) for m, a in sorted(enumerate(to_owners, 1), key=lambda pair: pair[0] != upper // 2)]

    w_groups = []
    for s in shifts:
        group = []
        for k in range((s - 1) * pieces, s * pieces):
            held_here = [first_w[k], hops[k]] if k in hops else [first_w[k]]
            group += held_here + [flip(after(a, gradients), 1) for a in held_here]
        w_groups.append(group)
    value_parts = []
    for s in shifts:
        value_part = call(
            other_values_kernel,
            [SMEM, VMEM] + [VMEM] * len(w_groups[s - 1]),
            [like((token_rows, values // HALVES), bf16)] * HALVES,
            [VMEM] * HALVES,
            (after(here, summed), inputs, *w_groups[s - 1]),
            flops=2 * token_rows * features * values,
            moved=2 * features * (token_rows + values),
            chunk=chunk,
        )
        value_parts += value_part

    flat = [w for group in w_groups for w in group]
    gradient_inputs = call(
        input_gradient_kernel,
        [SMEM] + [VMEM] * (3 + len(cots) + len(flat)),
        like((token_rows, features), bf16),
        VMEM,
        (after(here, *value_parts), gradient_own, grad_low, blocks, *cots, *flat),
        flops=2 * token_rows * features * values * len(cots),
        moved=2 * features * values * len(cots) + 4 * token_rows * features,
        groups=len(cots),
        parts=len(w_groups[0]),
        chunk=chunk,
    )
    returned = [turn(a, -(i // HALVES + 1)) for i, a in enumerate(value_parts)]
    adapted_values, down_grad, gradient_up_matrix = call(
        last_kernel,
        [VMEM] * (3 + len(returned)) + [SMEM, SMEM] + [VMEM] * upper,
        [
            like((token_rows, values), bf16),
            like((owned, RANK, features), f32),
            like((owned, RANK, values), f32),
        ],
        [VMEM] * 3,
        (value_own, low, blocks, *returned, here, quotas, summed, *owners),
        owned=owned,
        n_returned=len(returned),
    )
    return (adapted_values, gradient_inputs, jnp.swapaxes(down_grad, 1, 2), gradient_up_matrix)


def solution(mesh):
    placed = (
        P("dp", "tensor"),
        P(None, "tensor"),
        P("dp", "tensor", None),
        P("dp", None, "tensor"),
        P("dp", "tensor"),
        P("dp"),
        P(),
    )
    return jax.shard_map(
        on_device,
        mesh=mesh,
        in_specs=placed,
        out_specs=(
            P("dp", "tensor"),
            P("dp", "tensor"),
            P("dp", "tensor", None),
            P("dp", None, "tensor"),
        ),
        check_vma=False,
    )
```
